32 devices in a mesh: groups: 2 (over y), shard: 16 (over z, x, core).
Axes of the slice: x: 2, y: 2, z: 4, core: 2. Of those that a mesh axis runs over, the one named last changes fastest.
Arguments:
- hidden_states: bfloat16 [1024, 4096], P('groups', 'shard'), parts along dimension 0, may hold values from -6 to 6
- head_weight: bfloat16 [16384, 4096], P('shard'), may hold values from -0.09375 to 0.09375
- impact_tiles: bfloat16 [2048, 128, 128], P('shard'), may hold values from -0.23925781 to 0.23925781
- tile_active: int32 [16, 128], P('shard'), may hold values from 0 to 15, as said below
- tile_pblock: int32 [16, 128], P('shard'), may hold values from 0 to 15
- tile_count: int32 [16], P('shard'), may hold values from 1 to 128, as said below
- active_blocks: int32 [16, 16, 1], P('shard'), may hold values from 0 to 7
Outputs:
- scores: float32 [128, 32768], P('groups', 'shard'), parts along dimension 0
The draws below stay inside these ranges and needn't reach their ends.
There are 2 independent parts, one for each index of `groups`. The reference program is written for one: setup_inputs(seed, part) draws one part's arguments, and reference() takes and returns one part's arrays. A program takes and returns all parts, laid end to end along the dimension named above; an argument that names none is the same for every part. Nothing has to cross between parts.
Inputs may be any that keep to these rules, and one draw needn't show every extreme that they name: Slots at or beyond tile_count of a slab are padding; the busiest slab fills all 128 slots. `tile_active`: within one slab the first min(128, 16) slots name distinct entries.
All inputs are finite; a program needn't handle non-finite values.
Results may differ from the reference program's by a relative error of at most 0.003.
Values may be sent and summed in bfloat16 or wider, within the bound.
A program may use at most 128 MiB of HBM per device.

```python
import jax
import jax.numpy as jnp
from jax import lax

D = 4096
VB = 128
VBLK_DEV = 8
QLEN = 8
PB = 128
PBLK_DEV = 16
TILE_CAP = 128
REQ = 1
VOCAB = 16384
TOKENS = 512
ACTIVE = 16
N_SHARD = 16


def draw_tile_count(key, part):
    key = jax.random.fold_in(key, 11)
    first, second, third = jax.random.split(key, 3)
    counts = jax.random.randint(first, (N_SHARD,), TILE_CAP // 4, TILE_CAP // 2 + 1)
    busiest = jax.random.randint(second, (), 0, N_SHARD)
    other = (busiest + 1 + jax.random.randint(third, (), 0, N_SHARD - 1)) % N_SHARD
    counts = counts.at[other].set(TILE_CAP * 3 // 4)
    counts = counts.at[busiest].set(TILE_CAP)
    return counts.astype(jnp.int32)


def draw_tile_active(key, part):
    key = jax.random.fold_in(key, 23)
    keys = jax.random.split(key, N_SHARD)
    repeats = TILE_CAP // ACTIVE + 1

    def one_slab(slab_key):
        order = jax.random.permutation(slab_key, ACTIVE)
        return jnp.tile(order, repeats)[:TILE_CAP]
    return jax.vmap(one_slab)(keys).astype(jnp.int32)


def with_ends(result, stream_key, least, top_value):
    longest = result.shape.index(max(result.shape))
    spots = []
    for shift in (0, 1):
        where = [jax.random.randint(jax.random.fold_in(stream_key, axis), (), 0, length) for axis, length in enumerate(result.shape)]
        where[longest] = (where[longest] + shift) % result.shape[longest]
        spots.append(tuple(where))
    return result.at[spots[0]].set(least).at[spots[1]].set(top_value)


def block_levels(rng, shape, shards, smallest, top_value):
    loudness, own = 1.0, jax.random.fold_in(rng, 6)
    for axis_at, parts in shards:
        heights = jnp.exp(jax.random.uniform(jax.random.fold_in(own, axis_at), (parts,), jnp.float32, smallest / len(shards), top_value / len(shards)))
        loudness = loudness * jnp.repeat(heights, shape[axis_at] // parts).reshape([-1 if axis == axis_at else 1 for axis in range(len(shape))])
    return loudness


def scatter_about(stream_key, shape, deviation, most, shards=(), held_as=jnp.bfloat16):
    entries = jax.random.normal(stream_key, shape, jnp.float32) * deviation
    if len(shards) > 0:
        entries = block_levels(stream_key, shape, shards, -0.22, 0.18) * entries
    return jnp.clip(entries, min=-most, max=most).astype(held_as)


def setup_inputs(seed: int = 0, part: int = 0) -> dict:
    key_of = jax.random.split(jax.random.key(seed), 8)
    own_keys = jax.random.split(jax.random.fold_in(key_of[7], part), 8)
    hidden_states = scatter_about(own_keys[0], (TOKENS, D), 1.0, 6.0, ((1, 16),))
    head_weight = scatter_about(key_of[1], (VOCAB, D), D ** -0.5, 0.09375, ((0, 16),))
    impact_tiles = scatter_about(key_of[2], (N_SHARD * TILE_CAP, VB, PB), 0.03, 0.23925781, ((0, 16),))
    tile_active = draw_tile_active(jax.random.fold_in(key_of[7], 71), part)
    tile_pblock = with_ends(jax.random.randint(key_of[4], (N_SHARD, TILE_CAP), 0, PBLK_DEV), jax.random.fold_in(key_of[4], 1), 0, PBLK_DEV - 1).astype(jnp.int32)
    tile_count = draw_tile_count(jax.random.fold_in(key_of[7], 71), part)
    active_blocks = with_ends(jax.random.randint(key_of[6], (N_SHARD, N_SHARD, REQ), 0, VBLK_DEV), jax.random.fold_in(key_of[6], 1), 0, VBLK_DEV - 1).astype(jnp.int32)
    return {"hidden_states": hidden_states, "head_weight": head_weight, "impact_tiles": impact_tiles, "tile_active": tile_active, "tile_pblock": tile_pblock, "tile_count": tile_count, "active_blocks": active_blocks}


def reference(hidden_states, head_weight, impact_tiles, tile_active, tile_pblock, tile_count, active_blocks):
    logits = jnp.dot(hidden_states, head_weight.T, preferred_element_type=jnp.float32)
    queries = hidden_states.shape[0] // QLEN
    pooled = jnp.max(logits.reshape(queries, QLEN, logits.shape[1]), axis=1)
    term_weight = jnp.log1p(jnp.maximum(pooled, 0.0)).astype(jnp.bfloat16)
    block_total = term_weight.shape[1] // VB
    blocks = jnp.transpose(term_weight.reshape(queries, block_total, VB), (1, 0, 2))
    tiles = impact_tiles.reshape(N_SHARD, TILE_CAP, VB, PB)

    def one_slab(slab):
        owners = jnp.arange(N_SHARD, dtype=jnp.int32)[:, None] * VBLK_DEV
        global_ids = (owners + active_blocks[slab].astype(jnp.int32)).reshape(-1)
        table = jnp.take(blocks, global_ids, axis=0)
        chosen = jnp.take(table, tile_active[slab].astype(jnp.int32), axis=0)
        contrib = jnp.einsum("tqv,tvp->tqp", chosen.astype(jnp.float32), tiles[slab].astype(jnp.float32))
        slots = jnp.arange(TILE_CAP, dtype=jnp.int32)
        live = (slots < tile_count[slab]).astype(jnp.float32)
        onehot = (tile_pblock[slab][:, None] == jnp.arange(PBLK_DEV, dtype=jnp.int32)[None, :]).astype(jnp.float32)
        onehot = onehot * live[:, None]
        summed = jnp.einsum("tqp,tb->qbp", contrib, onehot, precision=lax.Precision.HIGHEST)
        return summed.reshape(queries, PBLK_DEV * PB)

    per_slab = lax.map(one_slab, jnp.arange(N_SHARD, dtype=jnp.int32))
    return jnp.transpose(per_slab, (1, 0, 2)).reshape(queries, N_SHARD * PBLK_DEV * PB)
```

```python
import functools
import math

import jax
import jax.numpy as jnp
from jax import lax
from jax.experimental import pallas as pl
from jax.experimental.pallas import tpu as pltpu
from jax.sharding import PartitionSpec as P

VB = 128
QLEN = 8
PB = 128
PBLK_DEV = 16
MESH = pl.DeviceIdType.MESH

NZ, NX, NC = 4, 2, 2
NDEV = NZ * NX * NC
F0, F1, G0, G1 = range(4)


def piece_rows(rows):
    f = rows * 9 // 32
    g = rows // 2 - f
    return ((0, f), (f, f), (2 * f, g), (2 * f + g, g))


def fused_kernel(
    rows,
    hs_ref, w_ref, tiles_ref, act_ref, cnt_ref, ab_ref, pb_ref, out_ref,
    hid, w_v, tiles_v, acc, tw, stage, table, pref, mine, wantv, chain_v, want_s, chain_s,
    send_sem, recv_sem, isend, irecv, xsend, xrecv, local_sem,
):
    me = lax.axis_index("shard")
    grp = lax.axis_index("groups")
    z, x, c = me // (NX * NC), (me // NC) % NX, me % NC
    pieces = piece_rows(rows)
    cols = hs_ref.shape[1]
    vocab = w_ref.shape[0]
    nblk = vocab // VB
    queries = rows // QLEN
    slots = tiles_ref.shape[0]

    def at(dz, dx, dc=0):
        return ((z + dz % NZ) % NZ) * (NX * NC) + ((x + dx) % NX) * NC + (c + dc) % NC

    own_copy = pltpu.make_async_copy(hs_ref, hid.at[me], local_sem.at[0])
    own_copy.start()
    w_copy = pltpu.make_async_copy(w_ref, w_v, local_sem.at[1])
    w_copy.start()

    barrier = pltpu.get_barrier_semaphore()
    for k in range(1, NDEV):
        pl.semaphore_signal(barrier, inc=1, device_id=(grp, (me + k) % NDEV), device_id_type=MESH)
    pl.semaphore_wait(barrier, NDEV - 1)

    sends = []

    def view(ref, blk, piece):
        start, size = pieces[piece]
        return ref.at[blk, pl.ds(start, size), :]

    def send(blk, piece, to, own=False):
        start, size = pieces[piece]
        src = hs_ref.at[pl.ds(start, size), :] if own else view(hid, blk, piece)
        copy = pltpu.make_async_remote_copy(
            src_ref=src,
            dst_ref=view(hid, blk, piece),
            send_sem=send_sem.at[len(sends)],
            recv_sem=recv_sem.at[blk, piece],
            device_id=(grp, to),
            device_id_type=MESH,
        )
        copy.start()
        sends.append(copy)

    def arrived(blk, piece):
        pltpu.make_async_remote_copy(
            src_ref=view(hid, blk, piece),
            dst_ref=view(hid, blk, piece),
            send_sem=send_sem.at[0],
            recv_sem=recv_sem.at[blk, piece],
            device_id=(grp, at(0, 0, 1)),
            device_id_type=MESH,
        ).wait_recv()

    zp, zm, xo, sib = at(1, 0), at(-1, 0), at(0, 1), at(0, 0, 1)
    for pz, mz, px in ((G0, G1, F0), (G1, G0, F1), (F0, F1, G0), (F1, F0, G1)):
        send(me, pz, zp, True)
        send(me, mz, zm, True)
        send(me, px, xo, True)
    for piece in range(4):
        send(me, piece, sib, True)

    tiles_copy = pltpu.make_async_copy(tiles_ref, tiles_v, local_sem.at[2])
    tiles_copy.start()

    isends = []
    for k in range(1, NDEV):
        owner = (me + k) % NDEV
        mine[k] = jnp.full((8, 128), ab_ref[0, owner, 0], jnp.int32)
        copy = pltpu.make_async_remote_copy(
            src_ref=mine.at[k],
            dst_ref=wantv.at[me],
            send_sem=isend.at[k],
            recv_sem=irecv.at[me],
            device_id=(grp, owner),
            device_id_type=MESH,
        )
        copy.start()
        isends.append(copy)
    wantv[me] = jnp.full((8, 128), ab_ref[0, me, 0], jnp.int32)

    sub = lax.broadcasted_iota(jnp.int32, (slots, slots), 0)
    lane = lax.broadcasted_iota(jnp.int32, (slots, slots), 1)
    pb_row = pb_ref[...]
    pb_col = jnp.sum(jnp.where(sub == lane, pb_row, 0), axis=1, keepdims=True)
    live = sub < cnt_ref[0]
    same = jnp.logical_and(jnp.logical_and(pb_col == pb_row, sub < lane), live)
    prev = jnp.max(jnp.where(same, sub + 1, 0), axis=0, keepdims=True)
    lasts = jnp.max(jnp.where(jnp.logical_and(pb_col == lane, live), sub + 1, 0), axis=0, keepdims=True)
    row8 = lax.broadcasted_iota(jnp.int32, (8, slots), 0)
    chain_v[...] = jnp.where(row8 == 0, prev, lasts)
    chain_copy = pltpu.make_async_copy(chain_v, chain_s, local_sem.at[3])
    chain_copy.start()
    pref[0] = jnp.zeros((queries, PB), jnp.float32)

    step_n = 256

    def product(blk, n):
        left = hid[blk]
        right = w_v[pl.ds(pl.multiple_of(n * step_n, step_n), step_n), pl.ds(pl.multiple_of(blk * cols, cols), cols)]
        return lax.dot_general(left, right, (((1,), (1,)), ((), ())), preferred_element_type=jnp.float32)

    def multiply(blk, first=False):
        @pl.loop(0, vocab // step_n)
        def _(n):
            where = pl.ds(pl.multiple_of(n * step_n, step_n), step_n)
            if first:
                acc[:, where] = product(blk, n)
            else:
                acc[:, where] += product(blk, n)

    def take(blk, piece, *to):
        arrived(blk, piece)
        for dev in to:
            send(blk, piece, dev)
        send(blk, piece, sib)

    def sibling(dz, dx):
        blk = at(dz, dx, 1)
        for piece in range(4):
            arrived(blk, piece)
        multiply(blk)

    b_zm, b_zp, b_x, b_zz = at(-1, 0), at(1, 0), at(0, 1), at(2, 0)
    d_zm, d_zp, d_zz = at(-1, 1), at(1, 1), at(2, 1)

    take(b_zm, G0, zp, xo)
    take(b_zp, G1, zm, xo)
    own_copy.wait()
    w_copy.wait()
    multiply(me, first=True)
    take(b_x, F0, zp, zm)
    take(b_zm, G1, xo)
    take(b_zp, G0, xo)
    sibling(0, 0)
    take(b_x, F1, zp, zm)
    take(b_zm, F0, zp)
    take(b_zp, F1, zm)
    take(b_x, G0)
    take(b_zm, F1)
    take(b_zp, F0)
    take(b_x, G1)
    multiply(b_zm)
    take(b_zz, G0, xo)
    take(b_zz, G1, xo)
    multiply(b_zp)
    take(d_zm, G0)
    take(d_zm, F0, zp)
    take(d_zp, F1, zm)
    multiply(b_x)
    sibling(-1, 0)
    take(d_zp, G1)
    take(d_zm, G1)
    take(d_zp, G0)
    sibling(1, 0)
    take(d_zm, F1)
    take(d_zp, F0)
    sibling(0, 1)
    multiply(d_zm)
    multiply(d_zp)

    for k in range(1, NDEV):
        other = (me + k) % NDEV
        pltpu.make_async_remote_copy(
            src_ref=mine.at[k], dst_ref=wantv.at[other], send_sem=isend.at[k],
            recv_sem=irecv.at[other], device_id=(grp, other), device_id_type=MESH,
        ).wait_recv()
    want_copy = pltpu.make_async_copy(wantv, want_s, local_sem.at[4])
    want_copy.start()

    take(b_zz, F0)
    take(b_zz, F1)
    take(d_zz, G0)
    take(d_zz, G1)
    sibling(-1, 1)
    sibling(1, 1)
    multiply(b_zz)
    take(d_zz, F0)
    take(d_zz, F1)
    sibling(2, 0)
    multiply(d_zz)
    want_copy.wait()
    chain_copy.wait()
    tiles_copy.wait()

    last = at(2, 1, 1)
    for piece in range(4):
        arrived(last, piece)

    @pl.loop(0, vocab // step_n)
    def _(n):
        where = pl.ds(pl.multiple_of(n * step_n, step_n), step_n)
        total = acc[:, where] + product(last, n)
        pooled = jnp.max(total.reshape(queries, QLEN, step_n), axis=1)
        weight = jnp.log1p(jnp.maximum(pooled, 0.0)).astype(jnp.bfloat16)
        for part in range(step_n // VB):
            tw[n * (step_n // VB) + part] = weight[:, part * VB:(part + 1) * VB]

    xsends = []
    for k in range(1, NDEV):
        slab = (me + k) % NDEV
        stage[k] = tw[want_s[slab, 0, 0]]
        copy = pltpu.make_async_remote_copy(
            src_ref=stage.at[k], dst_ref=table.at[me], send_sem=xsend.at[k],
            recv_sem=xrecv.at[me], device_id=(grp, slab), device_id_type=MESH,
        )
        copy.start()
        xsends.append(copy)
    table[me] = tw[want_s[me, 0, 0]]
    for k in range(1, NDEV):
        owner = (me + k) % NDEV
        pltpu.make_async_remote_copy(
            src_ref=stage.at[k], dst_ref=table.at[owner], send_sem=xsend.at[k],
            recv_sem=xrecv.at[owner], device_id=(grp, owner), device_id_type=MESH,
        ).wait_recv()

    unroll = 16

    @pl.loop(0, slots // unroll)
    def _(i):
        base = i * unroll
        parts = []
        for j in range(unroll):
            t = base + j
            parts.append(jnp.dot(table[act_ref[0, t]], tiles_v[t], preferred_element_type=jnp.float32))
        for j in range(unroll):
            t = base + j
            pref[t + 1] = pref[chain_s[0, t]] + parts[j]

    for b in range(PBLK_DEV):
        out_ref[:, b * PB:(b + 1) * PB] = pref[chain_s[1, b]]

    for copy in sends + isends + xsends:
        copy.wait_send()


def fused(hidden_states, head_weight, impact_tiles, tile_active, tile_pblock, tile_count, active_blocks):
    rows, cols = hidden_states.shape
    vocab, depth = head_weight.shape
    slots = impact_tiles.shape[0]
    queries = rows // QLEN
    hbm = pl.BlockSpec(memory_space=pl.ANY)
    smem = pl.BlockSpec(memory_space=pltpu.SMEM)
    vmem = pl.BlockSpec(memory_space=pltpu.VMEM)
    return pl.pallas_call(
        functools.partial(fused_kernel, rows),
        out_shape=jax.ShapeDtypeStruct((queries, PBLK_DEV * PB), jnp.float32),
        in_specs=[hbm, hbm, hbm, smem, smem, smem, vmem],
        out_specs=vmem,
        scratch_shapes=[
            pltpu.VMEM((NDEV, rows, cols), jnp.bfloat16),
            pltpu.VMEM((vocab, depth), jnp.bfloat16),
            pltpu.VMEM((slots, VB, PB), jnp.bfloat16),
            pltpu.VMEM((rows, vocab), jnp.float32),
            pltpu.VMEM((vocab // VB, queries, VB), jnp.bfloat16),
            pltpu.VMEM((NDEV, queries, VB), jnp.bfloat16),
            pltpu.VMEM((NDEV, queries, VB), jnp.bfloat16),
            pltpu.VMEM((slots + 1, queries, PB), jnp.float32),
            pltpu.VMEM((NDEV, 8, 128), jnp.int32),
            pltpu.VMEM((NDEV, 8, 128), jnp.int32),
            pltpu.VMEM((8, slots), jnp.int32),
            pltpu.SMEM((NDEV, 8, 128), jnp.int32),
            pltpu.SMEM((8, slots), jnp.int32),
            pltpu.SemaphoreType.DMA((64,)),
            pltpu.SemaphoreType.DMA((NDEV, 4)),
            pltpu.SemaphoreType.DMA((NDEV,)),
            pltpu.SemaphoreType.DMA((NDEV,)),
            pltpu.SemaphoreType.DMA((NDEV,)),
            pltpu.SemaphoreType.DMA((NDEV,)),
            pltpu.SemaphoreType.DMA((5,)),
        ],
        compiler_params=pltpu.CompilerParams(
            collective_id=0, has_side_effects=True, vmem_limit_bytes=44 * 1024 * 1024
        ),
        name="encode_and_score",
    )(hidden_states, head_weight, impact_tiles, tile_active, tile_count, active_blocks, tile_pblock)


def general(hidden_states, head_weight, impact_tiles, tile_active, tile_pblock, tile_count, active_blocks):
    token_rows = hidden_states.shape[0]
    vocab_rows = head_weight.shape[0]
    logits = lax.dot_general(
        lax.all_gather(hidden_states, "shard", axis=1, tiled=True),
        head_weight,
        (((1,), (1,)), ((), ())),
        preferred_element_type=jnp.float32,
    )
    queries = token_rows // QLEN
    pooled = jnp.max(logits.reshape(queries, QLEN, vocab_rows), axis=1)
    term_weight = jnp.log1p(jnp.maximum(pooled, 0.0)).astype(jnp.bfloat16)
    block_local = vocab_rows // VB
    blocks = jnp.transpose(term_weight.reshape(queries, block_local, VB), (1, 0, 2))
    owners = lax.axis_size("shard")
    wanted = active_blocks[0]
    everything = lax.all_gather(blocks, "shard", axis=0, tiled=True)
    offsets = jnp.arange(owners, dtype=jnp.int32)[:, None] * block_local
    table = jnp.take(everything, (offsets + wanted).reshape(-1), axis=0)
    slot_total = impact_tiles.shape[0]
    step_size = math.gcd(slot_total, 16)
    counted = tile_count[0]
    slot_entries = tile_active[0]
    slot_blocks = tile_pblock[0]
    block_ids = jnp.arange(PBLK_DEV, dtype=jnp.int32)

    def sweep_step(index, accum):
        begin = index * step_size
        entries = lax.dynamic_slice_in_dim(slot_entries, begin, step_size)
        targets = lax.dynamic_slice_in_dim(slot_blocks, begin, step_size)
        chosen = jnp.take(table, entries, axis=0)
        impacts = lax.dynamic_slice_in_dim(impact_tiles, begin, step_size, 0)
        contrib = jnp.einsum("tqv,tvp->tqp", chosen, impacts, preferred_element_type=jnp.float32)
        live = (begin + jnp.arange(step_size, dtype=jnp.int32) < counted).astype(jnp.float32)
        onehot = (targets[:, None] == block_ids[None, :]).astype(jnp.float32) * live[:, None]
        return accum + jnp.einsum("tqp,tb->qbp", contrib, onehot, precision=lax.Precision.HIGHEST)

    start_scores = jnp.zeros((queries, PBLK_DEV, PB), jnp.float32)
    trips = slot_total // step_size
    summed = lax.fori_loop(0, trips, sweep_step, start_scores)
    return summed.reshape(queries, PBLK_DEV * PB)


def per_device(hidden_states, head_weight, impact_tiles, tile_active, tile_pblock, tile_count, active_blocks):
    rows, cols = hidden_states.shape
    fits = (
        lax.axis_size("shard") == NDEV
        and rows == 512
        and cols % 128 == 0
        and head_weight.shape[0] % 256 == 0
        and impact_tiles.shape[0] == 128
        and active_blocks.shape[2] == 1
    )
    run = fused if fits else general
    return run(hidden_states, head_weight, impact_tiles, tile_active, tile_pblock, tile_count, active_blocks)


def solution(mesh):
    return jax.shard_map(
        per_device,
        mesh=mesh,
        in_specs=(
            P("groups", "shard"),
            P("shard", None),
            P("shard", None, None),
            P("shard", None),
            P("shard", None),
            P("shard"),
            P("shard", None, None),
        ),
        out_specs=P("groups", "shard"),
        check_vma=False,
    )
```

```python
import math

import jax
import jax.numpy as jnp
from jax import lax
from jax.experimental import pallas as pl
from jax.experimental.pallas import tpu as pltpu
from jax.sharding import PartitionSpec as P

VB = 128
QLEN = 8
PB = 128
PBLK_DEV = 16
MESH = pl.DeviceIdType.MESH

NZ, NX, NC = 4, 2, 2
NDEV = NZ * NX * NC
GROUPS = ((80, 144, 144, 144),)
GROUP_ROWS = sum(GROUPS[0])
PIECES = []
for sizes in GROUPS:
    PIECES.append([])
    for size in sizes:
        done = sum(n for group in PIECES for _, n in group)
        PIECES[-1].append((done, size))
NPIECE = len(GROUPS[0])
NSEND = 128


def fused_kernel(
    hs_ref, w_ref, tiles_ref, act_hbm, cnt_hbm, ab_hbm, pb_hbm, out_ref,
    hid, w_v, tiles_v, acc, tw, stage, table, pref, mine, wantv, chain_v, want_s, chain_s,
    act_ref, cnt_ref, ab_ref, pb_ref, send_sem, recv_sem, isend, irecv, xsend, xrecv, local_sem,
):
    me = lax.axis_index("shard")
    grp = lax.axis_index("groups")
    z, x, c = me // (NX * NC), (me // NC) % NX, me % NC
    cols = hs_ref.shape[1]
    vocab = w_ref.shape[0]
    nblk = vocab // VB
    gq = GROUP_ROWS // QLEN
    slots = tiles_ref.shape[0]

    def at(zz, dx, dc=0):
        return zz * (NX * NC) + ((x + dx) % NX) * NC + (c + dc) % NC

    small = [
        pltpu.make_async_copy(src, dst, local_sem.at[5 + i])
        for i, (src, dst) in enumerate(
            ((ab_hbm, ab_ref), (pb_hbm, pb_ref), (cnt_hbm, cnt_ref), (act_hbm, act_ref))
        )
    ]
    for copy in small:
        copy.start()
    own_copy = pltpu.make_async_copy(hs_ref, hid.at[me], local_sem.at[0])
    own_copy.start()
    w_copy = pltpu.make_async_copy(w_ref, w_v, local_sem.at[1])
    w_copy.start()

    barrier = pltpu.get_barrier_semaphore()
    for k in range(1, NDEV):
        pl.semaphore_signal(barrier, inc=1, device_id=(grp, (me + k) % NDEV), device_id_type=MESH)
    pl.semaphore_wait(barrier, NDEV - 1)

    sends = []
    isends = []
    has_up, has_down = z < NZ - 1, z > 0
    middle = jnp.logical_and(has_up, has_down)
    up, down = jnp.minimum(z + 1, NZ - 1), jnp.maximum(z - 1, 0)
    xo, sib = at(z, 1), at(z, 0, 1)

    def view(ref, blk, g, p):
        start, size = PIECES[g][p]
        return ref.at[blk, pl.ds(start, size), :]

    def send(blk, g, p, to, own=False, when=None):
        start, size = PIECES[g][p]
        copy = pltpu.make_async_remote_copy(
            src_ref=hs_ref.at[pl.ds(start, size), :] if own else view(hid, blk, g, p),
            dst_ref=view(hid, blk, g, p),
            send_sem=send_sem.at[len(sends)],
            recv_sem=recv_sem.at[blk, g * NPIECE + p],
            device_id=(grp, to),
            device_id_type=MESH,
        )
        sends.append((when, copy))
        if when is None:
            copy.start()
        else:
            pl.when(when)(copy.start)

    def arrived(blk, g, p):
        pltpu.make_async_remote_copy(
            src_ref=view(hid, blk, g, p),
            dst_ref=view(hid, blk, g, p),
            send_sem=send_sem.at[0],
            recv_sem=recv_sem.at[blk, g * NPIECE + p],
            device_id=(grp, sib),
            device_id_type=MESH,
        ).wait_recv()

    flip = z >= NZ // 2
    folded = jnp.where(flip, NZ - 1 - z, z)

    def near(j):
        n = jnp.where(folded > j, j, j + 1)
        return jnp.where(flip, NZ - 1 - n, n)

    nears = [near(j) for j in range(NZ - 1)]
    F, GS = 0, range(1, NPIECE)

    def send_own(g):
        send(me, g, F, xo, own=True)
        for p in GS:
            send(me, g, p, at(up, 0), own=True, when=has_up)
            send(me, g, p, at(down, 0), own=True, when=has_down)
            send(me, g, p, xo, own=True)
        send(me, g, F, at(up, 0), own=True, when=has_up)
        send(me, g, F, at(down, 0), own=True, when=has_down)
        for p in range(NPIECE):
            send(me, g, p, sib, own=True)

    def onward(zz, dx):
        return at(jnp.where(zz < z, up, down), dx)

    def take_column(g, zz):
        blk = at(zz, 0)
        for p in (*GS, F):
            arrived(blk, g, p)
            send(blk, g, p, onward(zz, 0), when=middle)
            if p != F:
                send(blk, g, p, xo)
            send(blk, g, p, sib)

    def take_partner(g):
        blk = at(z, 1)
        arrived(blk, g, F)
        send(blk, g, F, at(up, 0), when=has_up)
        send(blk, g, F, at(down, 0), when=has_down)
        send(blk, g, F, sib)
        for p in GS:
            arrived(blk, g, p)
            send(blk, g, p, sib)

    def take_cross_f(g, zz):
        blk = at(zz, 1)
        arrived(blk, g, F)
        send(blk, g, F, onward(zz, 0), when=middle)
        send(blk, g, F, sib)

    def take_cross_g(g, zz):
        blk = at(zz, 1)
        for p in GS:
            arrived(blk, g, p)
            send(blk, g, p, sib)

    step_n = 512

    def product(g, chip, n):
        total = None
        for core in range(NC):
            blk = chip * NC + core
            left = hid[blk, g * GROUP_ROWS:(g + 1) * GROUP_ROWS, :]
            right = w_v[pl.ds(pl.multiple_of(n * step_n, step_n), step_n), pl.ds(pl.multiple_of(blk * cols, cols), cols)]
            part = lax.dot_general(left, right, (((1,), (1,)), ((), ())), preferred_element_type=jnp.float32)
            total = part if total is None else total + part
        return total

    def wait_sibling(g, zz, dx):
        for p in range(NPIECE):
            arrived(at(zz, dx, 1), g, p)
        return zz * NX + (x + dx) % NX

    def multiply(g, zz, dx, first=False):
        chip = wait_sibling(g, zz, dx)

        @pl.loop(0, vocab // step_n)
        def _(n):
            where = pl.ds(pl.multiple_of(n * step_n, step_n), step_n)
            if first:
                acc[g, :, where] = product(g, chip, n)
            else:
                acc[g, :, where] += product(g, chip, n)

    def multiply_last(g, zz, dx):
        chip = wait_sibling(g, zz, dx)

        @pl.loop(0, vocab // step_n)
        def _(n):
            where = pl.ds(pl.multiple_of(n * step_n, step_n), step_n)
            total = acc[g, :, where] + product(g, chip, n)
            pooled = jnp.max(total.reshape(gq, QLEN, step_n), axis=1)
            weight = jnp.log1p(jnp.maximum(pooled, 0.0)).astype(jnp.bfloat16)
            for part in range(step_n // VB):
                tw[g, n * (step_n // VB) + part] = weight[:, part * VB:(part + 1) * VB]

    def send_weights(g):
        for k in range(1, NDEV):
            slab = (me + k) % NDEV
            stage[g, k] = tw[g, want_s[slab, 0, 0]]
            copy = pltpu.make_async_remote_copy(
                src_ref=stage.at[g, k], dst_ref=table.at[g, me], send_sem=xsend.at[g, k],
                recv_sem=xrecv.at[g, me], device_id=(grp, slab), device_id_type=MESH,
            )
            copy.start()
            isends.append(copy)
        table[g, me] = tw[g, want_s[me, 0, 0]]

    unroll = 16

    def score(g):
        for k in range(1, NDEV):
            owner = (me + k) % NDEV
            pltpu.make_async_remote_copy(
                src_ref=stage.at[g, k], dst_ref=table.at[g, owner], send_sem=xsend.at[g, k],
                recv_sem=xrecv.at[g, owner], device_id=(grp, owner), device_id_type=MESH,
            ).wait_recv()

        @pl.loop(0, slots // unroll)
        def _(i):
            base = i * unroll
            parts = []
            for j in range(unroll):
                t = base + j
                parts.append(jnp.dot(table[g, act_ref[0, t]], tiles_v[t], preferred_element_type=jnp.float32))
            for j in range(unroll):
                t = base + j
                pref[t + 1] = pref[chain_s[0, t]] + parts[j]

        for b in range(PBLK_DEV):
            out_ref[g * gq:(g + 1) * gq, b * PB:(b + 1) * PB] = pref[chain_s[1, b]]

    send_own(0)
    tiles_copy = pltpu.make_async_copy(tiles_ref, tiles_v, local_sem.at[2])
    tiles_copy.start()
    for copy in small:
        copy.wait()

    for k in range(1, NDEV):
        owner = (me + k) % NDEV
        mine[k] = jnp.full((1, 128), ab_ref[0, owner], jnp.int32)
        copy = pltpu.make_async_remote_copy(
            src_ref=mine.at[k],
            dst_ref=wantv.at[me],
            send_sem=isend.at[k],
            recv_sem=irecv.at[me],
            device_id=(grp, owner),
            device_id_type=MESH,
        )
        copy.start()
        isends.append(copy)
    wantv[me] = jnp.full((1, 128), ab_ref[0, me], jnp.int32)

    sub = lax.broadcasted_iota(jnp.int32, (slots, slots), 0)
    lane = lax.broadcasted_iota(jnp.int32, (slots, slots), 1)
    pb_row = pb_ref[...]
    pb_col = jnp.sum(jnp.where(sub == lane, pb_row, 0), axis=1, keepdims=True)
    live = sub < cnt_ref[0, 0]
    same = jnp.logical_and(jnp.logical_and(pb_col == pb_row, sub < lane), live)
    prev = jnp.max(jnp.where(same, sub + 1, 0), axis=0, keepdims=True)
    lasts = jnp.max(jnp.where(jnp.logical_and(pb_col == lane, live), sub + 1, 0), axis=0, keepdims=True)
    row8 = lax.broadcasted_iota(jnp.int32, (8, slots), 0)
    chain_v[...] = jnp.where(row8 == 0, prev, lasts)
    chain_copy = pltpu.make_async_copy(chain_v, chain_s, local_sem.at[3])
    chain_copy.start()
    pref[0] = jnp.zeros((gq, PB), jnp.float32)
    own_copy.wait()
    w_copy.wait()

    def opening(g):
        take_column(g, nears[0])
        take_partner(g)

    def middle_part(g):
        multiply(g, z, 0, first=True)
        take_column(g, nears[1])
        take_cross_f(g, nears[0])
        multiply(g, nears[0], 0)
        multiply(g, z, 1)
        take_cross_g(g, nears[0])

    def closing(g):
        take_column(g, nears[2])
        take_cross_f(g, nears[1])
        multiply(g, nears[1], 0)
        multiply(g, nears[0], 1)
        take_cross_g(g, nears[1])
        take_cross_f(g, nears[2])
        multiply(g, nears[2], 0)
        multiply(g, nears[1], 1)
        take_cross_g(g, nears[2])

    def weights(g):
        multiply_last(g, nears[2], 1)
        send_weights(g)

    def fetch_wants():
        for k in range(1, NDEV):
            other = (me + k) % NDEV
            pltpu.make_async_remote_copy(
                src_ref=mine.at[k], dst_ref=wantv.at[other], send_sem=isend.at[k],
                recv_sem=irecv.at[other], device_id=(grp, other), device_id_type=MESH,
            ).wait_recv()
        want_copy = pltpu.make_async_copy(wantv, want_s, local_sem.at[4])
        want_copy.start()
        want_copy.wait()

    ngroup = len(GROUPS)
    opening(0)
    for g in range(ngroup):
        more = g + 1 < ngroup
        if more:
            send_own(g + 1)
        middle_part(g)
        if g == 0:
            fetch_wants()
        if more:
            opening(g + 1)
        closing(g)
        weights(g)
    chain_copy.wait()
    tiles_copy.wait()
    for g in range(ngroup):
        score(g)

    for when, copy in sends:
        if when is None:
            copy.wait_send()
        else:
            pl.when(when)(copy.wait_send)
    for copy in isends:
        copy.wait_send()


def fused(hidden_states, head_weight, impact_tiles, tile_active, tile_pblock, tile_count, active_blocks):
    rows, cols = hidden_states.shape
    vocab, depth = head_weight.shape
    slots = impact_tiles.shape[0]
    queries = rows // QLEN
    ngroup, gq = len(GROUPS), GROUP_ROWS // QLEN
    hbm = pl.BlockSpec(memory_space=pl.ANY)
    vmem = pl.BlockSpec(memory_space=pltpu.VMEM)
    return pl.pallas_call(
        fused_kernel,
        out_shape=jax.ShapeDtypeStruct((queries, PBLK_DEV * PB), jnp.float32),
        in_specs=[hbm] * 7,
        out_specs=vmem,
        scratch_shapes=[
            pltpu.VMEM((NDEV, rows, cols), jnp.bfloat16),
            pltpu.VMEM((vocab, depth), jnp.bfloat16),
            pltpu.VMEM((slots, VB, PB), jnp.bfloat16),
            pltpu.VMEM((ngroup, GROUP_ROWS, vocab), jnp.float32),
            pltpu.VMEM((ngroup, vocab // VB, gq, VB), jnp.bfloat16),
            pltpu.VMEM((ngroup, NDEV, gq, VB), jnp.bfloat16),
            pltpu.VMEM((ngroup, NDEV, gq, VB), jnp.bfloat16),
            pltpu.VMEM((slots + 1, gq, PB), jnp.float32),
            pltpu.VMEM((NDEV, 1, 128), jnp.int32),
            pltpu.VMEM((NDEV, 1, 128), jnp.int32),
            pltpu.VMEM((8, slots), jnp.int32),
            pltpu.SMEM((NDEV, 1, 128), jnp.int32),
            pltpu.SMEM((8, slots), jnp.int32),
            pltpu.SMEM((1, slots), jnp.int32),
            pltpu.SMEM((1, 1), jnp.int32),
            pltpu.SMEM((1, NDEV), jnp.int32),
            pltpu.VMEM((1, slots), jnp.int32),
            pltpu.SemaphoreType.DMA((NSEND,)),
            pltpu.SemaphoreType.DMA((NDEV, ngroup * NPIECE)),
            pltpu.SemaphoreType.DMA((NDEV,)),
            pltpu.SemaphoreType.DMA((NDEV,)),
            pltpu.SemaphoreType.DMA((ngroup, NDEV)),
            pltpu.SemaphoreType.DMA((ngroup, NDEV)),
            pltpu.SemaphoreType.DMA((9,)),
        ],
        compiler_params=pltpu.CompilerParams(
            collective_id=0, has_side_effects=True, vmem_limit_bytes=60 * 1024 * 1024
        ),
        name="encode_and_score",
    )(
        hidden_states, head_weight, impact_tiles, tile_active, tile_count.reshape(1, 1),
        active_blocks.reshape(1, NDEV), tile_pblock,
    )


def general(hidden_states, head_weight, impact_tiles, tile_active, tile_pblock, tile_count, active_blocks):
    token_rows = hidden_states.shape[0]
    vocab_rows = head_weight.shape[0]
    logits = lax.dot_general(
        lax.all_gather(hidden_states, "shard", axis=1, tiled=True),
        head_weight,
        (((1,), (1,)), ((), ())),
        preferred_element_type=jnp.float32,
    )
    queries = token_rows // QLEN
    pooled = jnp.max(logits.reshape(queries, QLEN, vocab_rows), axis=1)
    term_weight = jnp.log1p(jnp.maximum(pooled, 0.0)).astype(jnp.bfloat16)
    block_local = vocab_rows // VB
    blocks = jnp.transpose(term_weight.reshape(queries, block_local, VB), (1, 0, 2))
    owners = lax.axis_size("shard")
    wanted = active_blocks[0]
    everything = lax.all_gather(blocks, "shard", axis=0, tiled=True)
    offsets = jnp.arange(owners, dtype=jnp.int32)[:, None] * block_local
    table = jnp.take(everything, (offsets + wanted).reshape(-1), axis=0)
    slot_total = impact_tiles.shape[0]
    step_size = math.gcd(slot_total, 16)
    counted = tile_count[0]
    slot_entries = tile_active[0]
    slot_blocks = tile_pblock[0]
    block_ids = jnp.arange(PBLK_DEV, dtype=jnp.int32)

    def sweep_step(index, accum):
        begin = index * step_size
        entries = lax.dynamic_slice_in_dim(slot_entries, begin, step_size)
        targets = lax.dynamic_slice_in_dim(slot_blocks, begin, step_size)
        chosen = jnp.take(table, entries, axis=0)
        impacts = lax.dynamic_slice_in_dim(impact_tiles, begin, step_size, 0)
        contrib = jnp.einsum("tqv,tvp->tqp", chosen, impacts, preferred_element_type=jnp.float32)
        live = (begin + jnp.arange(step_size, dtype=jnp.int32) < counted).astype(jnp.float32)
        onehot = (targets[:, None] == block_ids[None, :]).astype(jnp.float32) * live[:, None]
        return accum + jnp.einsum("tqp,tb->qbp", contrib, onehot, precision=lax.Precision.HIGHEST)

    start_scores = jnp.zeros((queries, PBLK_DEV, PB), jnp.float32)
    trips = slot_total // step_size
    summed = lax.fori_loop(0, trips, sweep_step, start_scores)
    return summed.reshape(queries, PBLK_DEV * PB)


def per_device(hidden_states, head_weight, impact_tiles, tile_active, tile_pblock, tile_count, active_blocks):
    rows, cols = hidden_states.shape
    fits = (
        lax.axis_size("shard") == NDEV
        and rows == len(GROUPS) * GROUP_ROWS
        and cols % 128 == 0
        and head_weight.shape[0] % 256 == 0
        and impact_tiles.shape[0] == 128
        and active_blocks.shape[2] == 1
    )
    run = fused if fits else general
    return run(hidden_states, head_weight, impact_tiles, tile_active, tile_pblock, tile_count, active_blocks)


def solution(mesh):
    return jax.shard_map(
        per_device,
        mesh=mesh,
        in_specs=(
            P("groups", "shard"),
            P("shard", None),
            P("shard", None, None),
            P("shard", None),
            P("shard", None),
            P("shard"),
            P("shard", None, None),
        ),
        out_specs=P("groups", "shard"),
        check_vma=False,
    )
```

```python
import math

import jax
import jax.numpy as jnp
from jax import lax
from jax.experimental import pallas as pl
from jax.experimental.pallas import tpu as pltpu
from jax.sharding import PartitionSpec as P

VB = 128
QLEN = 8
PB = 128
PBLK_DEV = 16
MESH = pl.DeviceIdType.MESH

NZ, NX, NC = 4, 2, 2
NDEV = NZ * NX * NC
GROUPS = ((80, 144, 144, 144),)
GROUP_ROWS = sum(GROUPS[0])
PIECES = []
for sizes in GROUPS:
    PIECES.append([])
    for size in sizes:
        done = sum(n for group in PIECES for _, n in group)
        PIECES[-1].append((done, size))
NPIECE = len(GROUPS[0])
NSEND = 128


def fused_kernel(
    hs_ref, w_ref, tiles_ref, act_hbm, cnt_hbm, ab_hbm, pb_hbm, out_ref,
    hid, w_v, tiles_v, acc, tw, stage, table, pref, mine, wantv, chain_v, want_s, chain_s,
    act_ref, cnt_ref, ab_ref, pb_ref, send_sem, recv_sem, isend, irecv, xsend, xrecv, local_sem,
):
    me = lax.axis_index("shard")
    grp = lax.axis_index("groups")
    z, x, c = me // (NX * NC), (me // NC) % NX, me % NC
    cols = hs_ref.shape[1]
    vocab = w_ref.shape[0]
    nblk = vocab // VB
    gq = GROUP_ROWS // QLEN
    slots = tiles_ref.shape[0]

    def at(zz, dx, dc=0):
        return zz * (NX * NC) + ((x + dx) % NX) * NC + (c + dc) % NC

    small = [
        pltpu.make_async_copy(src, dst, local_sem.at[5 + i])
        for i, (src, dst) in enumerate(
            ((ab_hbm, ab_ref), (pb_hbm, pb_ref), (cnt_hbm, cnt_ref), (act_hbm, act_ref))
        )
    ]
    for copy in small:
        copy.start()
    own_copy = pltpu.make_async_copy(hs_ref, hid.at[me], local_sem.at[0])
    own_copy.start()
    w_copy = pltpu.make_async_copy(w_ref, w_v, local_sem.at[1])
    w_copy.start()

    barrier = pltpu.get_barrier_semaphore()
    for k in range(1, NDEV):
        pl.semaphore_signal(barrier, inc=1, device_id=(grp, (me + k) % NDEV), device_id_type=MESH)
    pl.semaphore_wait(barrier, NDEV - 1)

    sends = []
    isends = []
    has_up, has_down = z < NZ - 1, z > 0
    middle = jnp.logical_and(has_up, has_down)
    up, down = jnp.minimum(z + 1, NZ - 1), jnp.maximum(z - 1, 0)
    xo, sib = at(z, 1), at(z, 0, 1)

    def view(ref, blk, g, p):
        start, size = PIECES[g][p]
        return ref.at[blk, pl.ds(start, size), :]

    def send(blk, g, p, to, own=False, when=None):
        start, size = PIECES[g][p]
        copy = pltpu.make_async_remote_copy(
            src_ref=hs_ref.at[pl.ds(start, size), :] if own else view(hid, blk, g, p),
            dst_ref=view(hid, blk, g, p),
            send_sem=send_sem.at[len(sends)],
            recv_sem=recv_sem.at[blk, g * NPIECE + p],
            device_id=(grp, to),
            device_id_type=MESH,
        )
        sends.append((when, copy))
        if when is None:
            copy.start()
        else:
            pl.when(when)(copy.start)

    def arrived(blk, g, p):
        pltpu.make_async_remote_copy(
            src_ref=view(hid, blk, g, p),
            dst_ref=view(hid, blk, g, p),
            send_sem=send_sem.at[0],
            recv_sem=recv_sem.at[blk, g * NPIECE + p],
            device_id=(grp, sib),
            device_id_type=MESH,
        ).wait_recv()

    flip = z >= NZ // 2
    folded = jnp.where(flip, NZ - 1 - z, z)

    def near(j):
        n = jnp.where(folded > j, j, j + 1)
        return jnp.where(flip, NZ - 1 - n, n)

    nears = [near(j) for j in range(NZ - 1)]
    F, GS = 0, range(1, NPIECE)

    def send_own(g):
        send(me, g, F, xo, own=True)
        for p in GS:
            send(me, g, p, at(up, 0), own=True, when=has_up)
            send(me, g, p, at(down, 0), own=True, when=has_down)
            send(me, g, p, xo, own=True)
        send(me, g, F, at(up, 0), own=True, when=has_up)
        send(me, g, F, at(down, 0), own=True, when=has_down)
        for p in range(NPIECE):
            send(me, g, p, sib, own=True)

    def onward(zz, dx):
        return at(jnp.where(zz < z, up, down), dx)

    def take_column(g, zz):
        blk = at(zz, 0)
        for p in (*GS, F):
            arrived(blk, g, p)
            send(blk, g, p, onward(zz, 0), when=middle)
            if p != F:
                send(blk, g, p, xo)
            send(blk, g, p, sib)

    def take_partner(g):
        blk = at(z, 1)
        arrived(blk, g, F)
        send(blk, g, F, at(up, 0), when=has_up)
        send(blk, g, F, at(down, 0), when=has_down)
        send(blk, g, F, sib)
        for p in GS:
            arrived(blk, g, p)
            send(blk, g, p, sib)

    def take_cross_f(g, zz):
        blk = at(zz, 1)
        arrived(blk, g, F)
        send(blk, g, F, onward(zz, 0), when=middle)
        send(blk, g, F, sib)

    def take_cross_g(g, zz):
        blk = at(zz, 1)
        for p in GS:
            arrived(blk, g, p)
            send(blk, g, p, sib)

    step_n = math.gcd(vocab, 1024)

    def product(g, chip, n):
        total = None
        for core in range(NC):
            blk = chip * NC + core
            left = hid[blk, g * GROUP_ROWS:(g + 1) * GROUP_ROWS, :]
            right = w_v[n * step_n:(n + 1) * step_n, pl.ds(pl.multiple_of(blk * cols, cols), cols)]
            part = lax.dot_general(left, right, (((1,), (1,)), ((), ())), preferred_element_type=jnp.float32)
            total = part if total is None else total + part
        return total

    def wait_sibling(g, zz, dx):
        for p in range(NPIECE):
            arrived(at(zz, dx, 1), g, p)
        return zz * NX + (x + dx) % NX

    def multiply(g, zz, dx, first=False):
        chip = wait_sibling(g, zz, dx)

        for n in range(vocab // step_n):
            where = slice(n * step_n, (n + 1) * step_n)
            if first:
                acc[g, :, where] = product(g, chip, n)
            else:
                acc[g, :, where] += product(g, chip, n)

    def multiply_last(g, zz, dx):
        chip = wait_sibling(g, zz, dx)

        for n in range(vocab // step_n):
            where = slice(n * step_n, (n + 1) * step_n)
            total = acc[g, :, where] + product(g, chip, n)
            pooled = jnp.max(total.reshape(gq, QLEN, step_n), axis=1)
            weight = jnp.log1p(jnp.maximum(pooled, 0.0)).astype(jnp.bfloat16)
            for part in range(step_n // VB):
                tw[g, n * (step_n // VB) + part] = weight[:, part * VB:(part + 1) * VB]

    def send_weights(g):
        for k in range(1, NDEV):
            slab = (me + k) % NDEV
            stage[g, k] = tw[g, want_s[slab, 0, 0]]
            copy = pltpu.make_async_remote_copy(
                src_ref=stage.at[g, k], dst_ref=table.at[g, me], send_sem=xsend.at[g, k],
                recv_sem=xrecv.at[g, me], device_id=(grp, slab), device_id_type=MESH,
            )
            copy.start()
            isends.append(copy)
        table[g, me] = tw[g, want_s[me, 0, 0]]

    unroll = 16

    def score(g):
        for k in range(1, NDEV):
            owner = (me + k) % NDEV
            pltpu.make_async_remote_copy(
                src_ref=stage.at[g, k], dst_ref=table.at[g, owner], send_sem=xsend.at[g, k],
                recv_sem=xrecv.at[g, owner], device_id=(grp, owner), device_id_type=MESH,
            ).wait_recv()

        @pl.loop(0, slots // unroll)
        def _(i):
            base = i * unroll
            parts = []
            for j in range(unroll):
                t = base + j
                parts.append(jnp.dot(table[g, act_ref[0, t]], tiles_v[t], preferred_element_type=jnp.float32))
            for j in range(unroll):
                t = base + j
                pref[t + 1] = pref[chain_s[0, t]] + parts[j]

        for b in range(PBLK_DEV):
            out_ref[g * gq:(g + 1) * gq, b * PB:(b + 1) * PB] = pref[chain_s[1, b]]

    send_own(0)
    for copy in small:
        copy.wait()

    for k in range(1, NDEV):
        owner = (me + k) % NDEV
        mine[k] = jnp.full((1, 128), ab_ref[0, owner], jnp.int32)
        copy = pltpu.make_async_remote_copy(
            src_ref=mine.at[k],
            dst_ref=wantv.at[me],
            send_sem=isend.at[k],
            recv_sem=irecv.at[me],
            device_id=(grp, owner),
            device_id_type=MESH,
        )
        copy.start()
        isends.append(copy)
    wantv[me] = jnp.full((1, 128), ab_ref[0, me], jnp.int32)

    sub = lax.broadcasted_iota(jnp.int32, (slots, slots), 0)
    lane = lax.broadcasted_iota(jnp.int32, (slots, slots), 1)
    pb_row = pb_ref[...]
    pb_col = jnp.sum(jnp.where(sub == lane, pb_row, 0), axis=1, keepdims=True)
    live = sub < cnt_ref[0, 0]
    same = jnp.logical_and(jnp.logical_and(pb_col == pb_row, sub < lane), live)
    prev = jnp.max(jnp.where(same, sub + 1, 0), axis=0, keepdims=True)
    lasts = jnp.max(jnp.where(jnp.logical_and(pb_col == lane, live), sub + 1, 0), axis=0, keepdims=True)
    row8 = lax.broadcasted_iota(jnp.int32, (8, slots), 0)
    chain_v[...] = jnp.where(row8 == 0, prev, lasts)
    chain_copy = pltpu.make_async_copy(chain_v, chain_s, local_sem.at[3])
    chain_copy.start()
    pref[0] = jnp.zeros((gq, PB), jnp.float32)

    def opening(g):
        take_column(g, nears[0])
        take_partner(g)

    def middle_part(g):
        multiply(g, z, 0, first=True)
        take_column(g, nears[1])
        take_cross_f(g, nears[0])
        multiply(g, nears[0], 0)
        multiply(g, z, 1)
        take_cross_g(g, nears[0])

    def closing(g):
        take_column(g, nears[2])
        take_cross_f(g, nears[1])
        multiply(g, nears[1], 0)
        multiply(g, nears[0], 1)
        take_cross_g(g, nears[1])
        take_cross_f(g, nears[2])
        multiply(g, nears[2], 0)
        multiply(g, nears[1], 1)
        take_cross_g(g, nears[2])

    def weights(g):
        multiply_last(g, nears[2], 1)
        send_weights(g)

    def fetch_wants():
        for k in range(1, NDEV):
            other = (me + k) % NDEV
            pltpu.make_async_remote_copy(
                src_ref=mine.at[k], dst_ref=wantv.at[other], send_sem=isend.at[k],
                recv_sem=irecv.at[other], device_id=(grp, other), device_id_type=MESH,
            ).wait_recv()
        want_copy = pltpu.make_async_copy(wantv, want_s, local_sem.at[4])
        want_copy.start()
        want_copy.wait()

    ngroup = len(GROUPS)
    opening(0)
    own_copy.wait()
    w_copy.wait()
    tiles_copy = pltpu.make_async_copy(tiles_ref, tiles_v, local_sem.at[2])
    tiles_copy.start()
    for g in range(ngroup):
        more = g + 1 < ngroup
        if more:
            send_own(g + 1)
        middle_part(g)
        if g == 0:
            fetch_wants()
        if more:
            opening(g + 1)
        closing(g)
        weights(g)
    chain_copy.wait()
    tiles_copy.wait()
    for g in range(ngroup):
        score(g)

    for when, copy in sends:
        if when is None:
            copy.wait_send()
        else:
            pl.when(when)(copy.wait_send)
    for copy in isends:
        copy.wait_send()


def fused(hidden_states, head_weight, impact_tiles, tile_active, tile_pblock, tile_count, active_blocks):
    rows, cols = hidden_states.shape
    vocab, depth = head_weight.shape
    slots = impact_tiles.shape[0]
    queries = rows // QLEN
    ngroup, gq = len(GROUPS), GROUP_ROWS // QLEN
    hbm = pl.BlockSpec(memory_space=pl.ANY)
    vmem = pl.BlockSpec(memory_space=pltpu.VMEM)
    return pl.pallas_call(
        fused_kernel,
        out_shape=jax.ShapeDtypeStruct((queries, PBLK_DEV * PB), jnp.float32),
        in_specs=[hbm] * 7,
        out_specs=vmem,
        scratch_shapes=[
            pltpu.VMEM((NDEV, rows, cols), jnp.bfloat16),
            pltpu.VMEM((vocab, depth), jnp.bfloat16),
            pltpu.VMEM((slots, VB, PB), jnp.bfloat16),
            pltpu.VMEM((ngroup, GROUP_ROWS, vocab), jnp.float32),
            pltpu.VMEM((ngroup, vocab // VB, gq, VB), jnp.bfloat16),
            pltpu.VMEM((ngroup, NDEV, gq, VB), jnp.bfloat16),
            pltpu.VMEM((ngroup, NDEV, gq, VB), jnp.bfloat16),
            pltpu.VMEM((slots + 1, gq, PB), jnp.float32),
            pltpu.VMEM((NDEV, 1, 128), jnp.int32),
            pltpu.VMEM((NDEV, 1, 128), jnp.int32),
            pltpu.VMEM((8, slots), jnp.int32),
            pltpu.SMEM((NDEV, 1, 128), jnp.int32),
            pltpu.SMEM((8, slots), jnp.int32),
            pltpu.SMEM((1, slots), jnp.int32),
            pltpu.SMEM((1, 1), jnp.int32),
            pltpu.SMEM((1, NDEV), jnp.int32),
            pltpu.VMEM((1, slots), jnp.int32),
            pltpu.SemaphoreType.DMA((NSEND,)),
            pltpu.SemaphoreType.DMA((NDEV, ngroup * NPIECE)),
            pltpu.SemaphoreType.DMA((NDEV,)),
            pltpu.SemaphoreType.DMA((NDEV,)),
            pltpu.SemaphoreType.DMA((ngroup, NDEV)),
            pltpu.SemaphoreType.DMA((ngroup, NDEV)),
            pltpu.SemaphoreType.DMA((9,)),
        ],
        compiler_params=pltpu.CompilerParams(
            collective_id=0, has_side_effects=True, vmem_limit_bytes=60 * 1024 * 1024
        ),
        name="encode_and_score",
    )(
        hidden_states, head_weight, impact_tiles, tile_active, tile_count.reshape(1, 1),
        active_blocks.reshape(1, NDEV), tile_pblock,
    )


def general(hidden_states, head_weight, impact_tiles, tile_active, tile_pblock, tile_count, active_blocks):
    token_rows = hidden_states.shape[0]
    vocab_rows = head_weight.shape[0]
    logits = lax.dot_general(
        lax.all_gather(hidden_states, "shard", axis=1, tiled=True),
        head_weight,
        (((1,), (1,)), ((), ())),
        preferred_element_type=jnp.float32,
    )
    queries = token_rows // QLEN
    pooled = jnp.max(logits.reshape(queries, QLEN, vocab_rows), axis=1)
    term_weight = jnp.log1p(jnp.maximum(pooled, 0.0)).astype(jnp.bfloat16)
    block_local = vocab_rows // VB
    blocks = jnp.transpose(term_weight.reshape(queries, block_local, VB), (1, 0, 2))
    owners = lax.axis_size("shard")
    wanted = active_blocks[0]
    everything = lax.all_gather(blocks, "shard", axis=0, tiled=True)
    offsets = jnp.arange(owners, dtype=jnp.int32)[:, None] * block_local
    table = jnp.take(everything, (offsets + wanted).reshape(-1), axis=0)
    slot_total = impact_tiles.shape[0]
    step_size = math.gcd(slot_total, 16)
    counted = tile_count[0]
    slot_entries = tile_active[0]
    slot_blocks = tile_pblock[0]
    block_ids = jnp.arange(PBLK_DEV, dtype=jnp.int32)

    def sweep_step(index, accum):
        begin = index * step_size
        entries = lax.dynamic_slice_in_dim(slot_entries, begin, step_size)
        targets = lax.dynamic_slice_in_dim(slot_blocks, begin, step_size)
        chosen = jnp.take(table, entries, axis=0)
        impacts = lax.dynamic_slice_in_dim(impact_tiles, begin, step_size, 0)
        contrib = jnp.einsum("tqv,tvp->tqp", chosen, impacts, preferred_element_type=jnp.float32)
        live = (begin + jnp.arange(step_size, dtype=jnp.int32) < counted).astype(jnp.float32)
        onehot = (targets[:, None] == block_ids[None, :]).astype(jnp.float32) * live[:, None]
        return accum + jnp.einsum("tqp,tb->qbp", contrib, onehot, precision=lax.Precision.HIGHEST)

    start_scores = jnp.zeros((queries, PBLK_DEV, PB), jnp.float32)
    trips = slot_total // step_size
    summed = lax.fori_loop(0, trips, sweep_step, start_scores)
    return summed.reshape(queries, PBLK_DEV * PB)


def per_device(hidden_states, head_weight, impact_tiles, tile_active, tile_pblock, tile_count, active_blocks):
    rows, cols = hidden_states.shape
    fits = (
        lax.axis_size("shard") == NDEV
        and rows == len(GROUPS) * GROUP_ROWS
        and cols % 128 == 0
        and head_weight.shape[0] % 256 == 0
        and impact_tiles.shape[0] == 128
        and active_blocks.shape[2] == 1
    )
    run = fused if fits else general
    return run(hidden_states, head_weight, impact_tiles, tile_active, tile_pblock, tile_count, active_blocks)


def solution(mesh):
    return jax.shard_map(
        per_device,
        mesh=mesh,
        in_specs=(
            P("groups", "shard"),
            P("shard", None),
            P("shard", None, None),
            P("shard", None),
            P("shard", None),
            P("shard"),
            P("shard", None, None),
        ),
        out_specs=P("groups", "shard"),
        check_vma=False,
    )
```

```python
import math

import jax
import jax.numpy as jnp
from jax import lax
from jax.experimental import pallas as pl
from jax.experimental.pallas import tpu as pltpu
from jax.sharding import PartitionSpec as P

VB = 128
QLEN = 8
PB = 128
PBLK_DEV = 16
MESH = pl.DeviceIdType.MESH

NZ, NX, NC = 4, 2, 2
NDEV = NZ * NX * NC
GROUPS = ((80, 144, 144, 144),)
GROUP_ROWS = sum(GROUPS[0])
PIECES = []
for sizes in GROUPS:
    PIECES.append([])
    for size in sizes:
        done = sum(n for group in PIECES for _, n in group)
        PIECES[-1].append((done, size))
NPIECE = len(GROUPS[0])
NSEND = 128


def fused_kernel(
    hs_ref, w_ref, tiles_ref, act_hbm, cnt_hbm, ab_hbm, pb_hbm, out_ref,
    hid, w_v, tiles_v, acc, tw, stage, table, pref, mine, wantv, chain_v, want_s, chain_s,
    act_ref, cnt_ref, ab_ref, pb_ref, out_v, send_sem, recv_sem, isend, irecv, xsend, xrecv, local_sem,
):
    me = lax.axis_index("shard")
    grp = lax.axis_index("groups")
    z, x, c = me // (NX * NC), (me // NC) % NX, me % NC
    cols = hs_ref.shape[1]
    vocab = w_ref.shape[0]
    nblk = vocab // VB
    gq = GROUP_ROWS // QLEN
    slots = tiles_ref.shape[0]

    def at(zz, dx, dc=0):
        return zz * (NX * NC) + ((x + dx) % NX) * NC + (c + dc) % NC

    small = [
        pltpu.make_async_copy(src, dst, local_sem.at[5 + i])
        for i, (src, dst) in enumerate(
            ((ab_hbm, ab_ref), (pb_hbm, pb_ref), (cnt_hbm, cnt_ref), (act_hbm, act_ref))
        )
    ]
    for copy in small:
        copy.start()
    own_copy = pltpu.make_async_copy(hs_ref, hid.at[me], local_sem.at[0])
    own_copy.start()
    w_copy = pltpu.make_async_copy(w_ref, w_v, local_sem.at[1])
    w_copy.start()

    barrier = pltpu.get_barrier_semaphore()
    for k in range(1, NDEV):
        pl.semaphore_signal(barrier, inc=1, device_id=(grp, (me + k) % NDEV), device_id_type=MESH)
    pl.semaphore_wait(barrier, NDEV - 1)

    sends = []
    isends = []
    has_up, has_down = z < NZ - 1, z > 0
    middle = jnp.logical_and(has_up, has_down)
    up, down = jnp.minimum(z + 1, NZ - 1), jnp.maximum(z - 1, 0)
    xo, sib = at(z, 1), at(z, 0, 1)

    def view(ref, blk, g, p):
        start, size = PIECES[g][p]
        return ref.at[blk, pl.ds(start, size), :]

    def send(blk, g, p, to, own=False, when=None):
        start, size = PIECES[g][p]
        copy = pltpu.make_async_remote_copy(
            src_ref=hs_ref.at[pl.ds(start, size), :] if own else view(hid, blk, g, p),
            dst_ref=view(hid, blk, g, p),
            send_sem=send_sem.at[len(sends)],
            recv_sem=recv_sem.at[blk, g * NPIECE + p],
            device_id=(grp, to),
            device_id_type=MESH,
        )
        sends.append((when, copy))
        if when is None:
            copy.start()
        else:
            pl.when(when)(copy.start)

    def arrived(blk, g, p):
        pltpu.make_async_remote_copy(
            src_ref=view(hid, blk, g, p),
            dst_ref=view(hid, blk, g, p),
            send_sem=send_sem.at[0],
            recv_sem=recv_sem.at[blk, g * NPIECE + p],
            device_id=(grp, sib),
            device_id_type=MESH,
        ).wait_recv()

    flip = z >= NZ // 2
    folded = jnp.where(flip, NZ - 1 - z, z)

    def near(j):
        n = jnp.where(folded > j, j, j + 1)
        return jnp.where(flip, NZ - 1 - n, n)

    nears = [near(j) for j in range(NZ - 1)]
    F, GS = 0, range(1, NPIECE)

    def send_own(g):
        send(me, g, F, xo, own=True)
        for p in GS:
            send(me, g, p, at(up, 0), own=True, when=has_up)
            send(me, g, p, at(down, 0), own=True, when=has_down)
            send(me, g, p, xo, own=True)
        send(me, g, F, at(up, 0), own=True, when=has_up)
        send(me, g, F, at(down, 0), own=True, when=has_down)
        for p in range(NPIECE):
            send(me, g, p, sib, own=True)

    def onward(zz, dx):
        return at(jnp.where(zz < z, up, down), dx)

    def take_column(g, zz):
        blk = at(zz, 0)
        for p in (*GS, F):
            arrived(blk, g, p)
            send(blk, g, p, onward(zz, 0), when=middle)
            if p != F:
                send(blk, g, p, xo)
            send(blk, g, p, sib)

    def take_partner(g):
        blk = at(z, 1)
        arrived(blk, g, F)
        send(blk, g, F, at(up, 0), when=has_up)
        send(blk, g, F, at(down, 0), when=has_down)
        send(blk, g, F, sib)
        for p in GS:
            arrived(blk, g, p)
            send(blk, g, p, sib)

    def take_cross_f(g, zz):
        blk = at(zz, 1)
        arrived(blk, g, F)
        send(blk, g, F, onward(zz, 0), when=middle)
        send(blk, g, F, sib)

    def take_cross_g(g, zz):
        blk = at(zz, 1)
        for p in GS:
            arrived(blk, g, p)
            send(blk, g, p, sib)

    step_n = math.gcd(vocab, 1024)

    def product(g, chip, n):
        total = None
        for core in range(NC):
            blk = chip * NC + core
            left = hid[blk, g * GROUP_ROWS:(g + 1) * GROUP_ROWS, :]
            right = w_v[n * step_n:(n + 1) * step_n, pl.ds(pl.multiple_of(blk * cols, cols), cols)]
            part = lax.dot_general(left, right, (((1,), (1,)), ((), ())), preferred_element_type=jnp.float32)
            total = part if total is None else total + part
        return total

    def wait_sibling(g, zz, dx):
        for p in range(NPIECE):
            arrived(at(zz, dx, 1), g, p)
        return zz * NX + (x + dx) % NX

    def multiply(g, zz, dx, first=False):
        chip = wait_sibling(g, zz, dx)

        for n in range(vocab // step_n):
            where = slice(n * step_n, (n + 1) * step_n)
            if first:
                acc[g, :, where] = product(g, chip, n)
            else:
                acc[g, :, where] += product(g, chip, n)

    def multiply_last(g, zz, dx):
        chip = wait_sibling(g, zz, dx)

        for n in range(vocab // step_n):
            where = slice(n * step_n, (n + 1) * step_n)
            total = acc[g, :, where] + product(g, chip, n)
            pooled = jnp.max(total.reshape(gq, QLEN, step_n), axis=1)
            weight = jnp.log1p(jnp.maximum(pooled, 0.0)).astype(jnp.bfloat16)
            for part in range(step_n // VB):
                tw[g, n * (step_n // VB) + part] = weight[:, part * VB:(part + 1) * VB]

    def send_weights(g):
        for k in range(1, NDEV):
            slab = (me + k) % NDEV
            stage[g, k] = tw[g, want_s[slab, 0, 0]]
            copy = pltpu.make_async_remote_copy(
                src_ref=stage.at[g, k], dst_ref=table.at[g, me], send_sem=xsend.at[g, k],
                recv_sem=xrecv.at[g, me], device_id=(grp, slab), device_id_type=MESH,
            )
            copy.start()
            isends.append(copy)
        table[g, me] = tw[g, want_s[me, 0, 0]]

    unroll = 16
    outs = []

    def score(g):
        for k in range(1, NDEV):
            owner = (me + k) % NDEV
            pltpu.make_async_remote_copy(
                src_ref=stage.at[g, k], dst_ref=table.at[g, owner], send_sem=xsend.at[g, k],
                recv_sem=xrecv.at[g, owner], device_id=(grp, owner), device_id_type=MESH,
            ).wait_recv()

        @pl.loop(0, slots // unroll)
        def _(i):
            base = i * unroll
            parts = []
            for j in range(unroll):
                t = base + j
                parts.append(jnp.dot(table[g, act_ref[0, t]], tiles_v[t], preferred_element_type=jnp.float32))
            for j in range(unroll):
                t = base + j
                pref[t + 1] = pref[chain_s[0, t]] + parts[j]

        for b in range(PBLK_DEV):
            out_v[b] = pref[chain_s[1, b]]
            if b % 4 == 3:
                part = pl.ds(b - 3, 4)
                copy = pltpu.make_async_copy(out_v.at[part], out_ref.at[part], local_sem.at[9 + b // 4])
                copy.start()
                outs.append(copy)

    send_own(0)
    for copy in small:
        copy.wait()

    for k in range(1, NDEV):
        owner = (me + k) % NDEV
        mine[k] = jnp.full((1, 128), ab_ref[0, owner], jnp.int32)
        copy = pltpu.make_async_remote_copy(
            src_ref=mine.at[k],
            dst_ref=wantv.at[me],
            send_sem=isend.at[k],
            recv_sem=irecv.at[me],
            device_id=(grp, owner),
            device_id_type=MESH,
        )
        copy.start()
        isends.append(copy)
    wantv[me] = jnp.full((1, 128), ab_ref[0, me], jnp.int32)

    sub = lax.broadcasted_iota(jnp.int32, (slots, slots), 0)
    lane = lax.broadcasted_iota(jnp.int32, (slots, slots), 1)
    pb_row = pb_ref[...]
    pb_col = jnp.sum(jnp.where(sub == lane, pb_row, 0), axis=1, keepdims=True)
    live = sub < cnt_ref[0, 0]
    same = jnp.logical_and(jnp.logical_and(pb_col == pb_row, sub < lane), live)
    prev = jnp.max(jnp.where(same, sub + 1, 0), axis=0, keepdims=True)
    lasts = jnp.max(jnp.where(jnp.logical_and(pb_col == lane, live), sub + 1, 0), axis=0, keepdims=True)
    row8 = lax.broadcasted_iota(jnp.int32, (8, slots), 0)
    chain_v[...] = jnp.where(row8 == 0, prev, lasts)
    chain_copy = pltpu.make_async_copy(chain_v, chain_s, local_sem.at[3])
    chain_copy.start()
    pref[0] = jnp.zeros((gq, PB), jnp.float32)

    def opening(g):
        take_column(g, nears[0])
        take_partner(g)

    def middle_part(g):
        multiply(g, z, 0, first=True)
        take_column(g, nears[1])
        take_cross_f(g, nears[0])
        multiply(g, nears[0], 0)
        multiply(g, z, 1)
        take_cross_g(g, nears[0])

    def closing(g):
        take_column(g, nears[2])
        take_cross_f(g, nears[1])
        multiply(g, nears[1], 0)
        multiply(g, nears[0], 1)
        take_cross_g(g, nears[1])
        take_cross_f(g, nears[2])
        multiply(g, nears[2], 0)
        multiply(g, nears[1], 1)
        take_cross_g(g, nears[2])

    def weights(g):
        multiply_last(g, nears[2], 1)
        send_weights(g)

    def fetch_wants():
        for k in range(1, NDEV):
            other = (me + k) % NDEV
            pltpu.make_async_remote_copy(
                src_ref=mine.at[k], dst_ref=wantv.at[other], send_sem=isend.at[k],
                recv_sem=irecv.at[other], device_id=(grp, other), device_id_type=MESH,
            ).wait_recv()
        want_copy = pltpu.make_async_copy(wantv, want_s, local_sem.at[4])
        want_copy.start()
        want_copy.wait()

    ngroup = len(GROUPS)
    opening(0)
    own_copy.wait()
    w_copy.wait()
    tiles_copy = pltpu.make_async_copy(tiles_ref, tiles_v, local_sem.at[2])
    tiles_copy.start()
    for g in range(ngroup):
        more = g + 1 < ngroup
        if more:
            send_own(g + 1)
        middle_part(g)
        if g == 0:
            fetch_wants()
        if more:
            opening(g + 1)
        closing(g)
        weights(g)
    chain_copy.wait()
    tiles_copy.wait()
    for g in range(ngroup):
        score(g)

    for when, copy in sends:
        if when is None:
            copy.wait_send()
        else:
            pl.when(when)(copy.wait_send)
    for copy in isends:
        copy.wait_send()
    for copy in outs:
        copy.wait()


def fused(hidden_states, head_weight, impact_tiles, tile_active, tile_pblock, tile_count, active_blocks):
    rows, cols = hidden_states.shape
    vocab, depth = head_weight.shape
    slots = impact_tiles.shape[0]
    queries = rows // QLEN
    ngroup, gq = len(GROUPS), GROUP_ROWS // QLEN
    hbm = pl.BlockSpec(memory_space=pl.ANY)
    scores = pl.pallas_call(
        fused_kernel,
        out_shape=jax.ShapeDtypeStruct((PBLK_DEV, queries, PB), jnp.float32),
        in_specs=[hbm] * 7,
        out_specs=hbm,
        scratch_shapes=[
            pltpu.VMEM((NDEV, rows, cols), jnp.bfloat16),
            pltpu.VMEM((vocab, depth), jnp.bfloat16),
            pltpu.VMEM((slots, VB, PB), jnp.bfloat16),
            pltpu.VMEM((ngroup, GROUP_ROWS, vocab), jnp.float32),
            pltpu.VMEM((ngroup, vocab // VB, gq, VB), jnp.bfloat16),
            pltpu.VMEM((ngroup, NDEV, gq, VB), jnp.bfloat16),
            pltpu.VMEM((ngroup, NDEV, gq, VB), jnp.bfloat16),
            pltpu.VMEM((slots + 1, gq, PB), jnp.float32),
            pltpu.VMEM((NDEV, 1, 128), jnp.int32),
            pltpu.VMEM((NDEV, 1, 128), jnp.int32),
            pltpu.VMEM((8, slots), jnp.int32),
            pltpu.SMEM((NDEV, 1, 128), jnp.int32),
            pltpu.SMEM((8, slots), jnp.int32),
            pltpu.SMEM((1, slots), jnp.int32),
            pltpu.SMEM((1, 1), jnp.int32),
            pltpu.SMEM((1, NDEV), jnp.int32),
            pltpu.VMEM((1, slots), jnp.int32),
            pltpu.VMEM((PBLK_DEV, queries, PB), jnp.float32),
            pltpu.SemaphoreType.DMA((NSEND,)),
            pltpu.SemaphoreType.DMA((NDEV, ngroup * NPIECE)),
            pltpu.SemaphoreType.DMA((NDEV,)),
            pltpu.SemaphoreType.DMA((NDEV,)),
            pltpu.SemaphoreType.DMA((ngroup, NDEV)),
            pltpu.SemaphoreType.DMA((ngroup, NDEV)),
            pltpu.SemaphoreType.DMA((13,)),
        ],
        compiler_params=pltpu.CompilerParams(
            collective_id=0, has_side_effects=True, vmem_limit_bytes=60 * 1024 * 1024
        ),
        name="encode_and_score",
    )(
        hidden_states, head_weight, impact_tiles, tile_active, tile_count.reshape(1, 1),
        active_blocks.reshape(1, NDEV), tile_pblock,
    )
    return jnp.transpose(scores, (1, 0, 2)).reshape(queries, PBLK_DEV * PB)


def general(hidden_states, head_weight, impact_tiles, tile_active, tile_pblock, tile_count, active_blocks):
    token_rows = hidden_states.shape[0]
    vocab_rows = head_weight.shape[0]
    logits = lax.dot_general(
        lax.all_gather(hidden_states, "shard", axis=1, tiled=True),
        head_weight,
        (((1,), (1,)), ((), ())),
        preferred_element_type=jnp.float32,
    )
    queries = token_rows // QLEN
    pooled = jnp.max(logits.reshape(queries, QLEN, vocab_rows), axis=1)
    term_weight = jnp.log1p(jnp.maximum(pooled, 0.0)).astype(jnp.bfloat16)
    block_local = vocab_rows // VB
    blocks = jnp.transpose(term_weight.reshape(queries, block_local, VB), (1, 0, 2))
    owners = lax.axis_size("shard")
    wanted = active_blocks[0]
    everything = lax.all_gather(blocks, "shard", axis=0, tiled=True)
    offsets = jnp.arange(owners, dtype=jnp.int32)[:, None] * block_local
    table = jnp.take(everything, (offsets + wanted).reshape(-1), axis=0)
    slot_total = impact_tiles.shape[0]
    step_size = math.gcd(slot_total, 16)
    counted = tile_count[0]
    slot_entries = tile_active[0]
    slot_blocks = tile_pblock[0]
    block_ids = jnp.arange(PBLK_DEV, dtype=jnp.int32)

    def sweep_step(index, accum):
        begin = index * step_size
        entries = lax.dynamic_slice_in_dim(slot_entries, begin, step_size)
        targets = lax.dynamic_slice_in_dim(slot_blocks, begin, step_size)
        chosen = jnp.take(table, entries, axis=0)
        impacts = lax.dynamic_slice_in_dim(impact_tiles, begin, step_size, 0)
        contrib = jnp.einsum("tqv,tvp->tqp", chosen, impacts, preferred_element_type=jnp.float32)
        live = (begin + jnp.arange(step_size, dtype=jnp.int32) < counted).astype(jnp.float32)
        onehot = (targets[:, None] == block_ids[None, :]).astype(jnp.float32) * live[:, None]
        return accum + jnp.einsum("tqp,tb->qbp", contrib, onehot, precision=lax.Precision.HIGHEST)

    start_scores = jnp.zeros((queries, PBLK_DEV, PB), jnp.float32)
    trips = slot_total // step_size
    summed = lax.fori_loop(0, trips, sweep_step, start_scores)
    return summed.reshape(queries, PBLK_DEV * PB)


def per_device(hidden_states, head_weight, impact_tiles, tile_active, tile_pblock, tile_count, active_blocks):
    rows, cols = hidden_states.shape
    fits = (
        lax.axis_size("shard") == NDEV
        and rows == len(GROUPS) * GROUP_ROWS
        and cols % 128 == 0
        and head_weight.shape[0] % 256 == 0
        and impact_tiles.shape[0] == 128
        and active_blocks.shape[2] == 1
    )
    run = fused if fits else general
    return run(hidden_states, head_weight, impact_tiles, tile_active, tile_pblock, tile_count, active_blocks)


def solution(mesh):
    return jax.shard_map(
        per_device,
        mesh=mesh,
        in_specs=(
            P("groups", "shard"),
            P("shard", None),
            P("shard", None, None),
            P("shard", None),
            P("shard", None),
            P("shard"),
            P("shard", None, None),
        ),
        out_specs=P("groups", "shard"),
        check_vma=False,
    )
```
